256 devices in a mesh: dp: 16 (over z, core), context: 16 (over x, y).
Axes of the slice: x: 4, y: 4, z: 8, core: 2. Of those that a mesh axis runs over, the one named last changes fastest.
Arguments:
- layer_input: bfloat16 [16, 2048, 8192], P('dp', 'context'), may hold values from -150 to 150
- value_weight: bfloat16 [8192, 512], replicated, may hold values from -0.0625 to 0.0625
- queries: bfloat16 [16, 2048, 4096], P('dp', 'context'), may hold values from -150 to 150
- key_states: bfloat16 [16, 2048, 512], P('dp', 'context'), may hold values from -6 to 6
- out_grads: bfloat16 [16, 2048, 4096], P('dp', 'context'), may hold values from -16 to 16
- lengths: int32 [16], P('dp'), may hold values from 0 to 2048, as said below
Outputs:
- clipped_sum: float32 [8192, 512], P('context', 'dp')
- doc_norms: float32 [16], P('dp')
- key_grads: bfloat16 [16, 2048, 512], P('dp', 'context')
The draws below stay inside these ranges and needn't reach their ends.
Inputs may be any that keep to these rules, and one draw needn't show every extreme that they name: `lengths`: a slot's document fills the slot's first positions; in every draw some slot is empty and some slot is full.
All inputs are finite; a program needn't handle non-finite values.
Results may differ from the reference program's by a relative error of at most 0.02.
Values may be sent and summed in bfloat16 or wider, within the bound.
A program may use at most 128 MiB of HBM per device.

```python
import math
import jax
import jax.numpy as jnp
from jax import lax

D = 8192
HD = 128
QH = 32
KVH = 4
SEQ = 2048
SLOTS = 16


def query_key_pair(key):
    seeds = jax.random.split(jax.random.fold_in(key, 7101), 2)
    key_shape = (SLOTS, SEQ, KVH, HD)
    query_shape = (SLOTS, SEQ, QH, HD)
    key_values = jnp.clip(jax.random.normal(seeds[0], key_shape, jnp.float32), -5.0, 5.0)
    query_values = jnp.clip(jax.random.normal(seeds[1], query_shape, jnp.float32), -5.0, 5.0)
    return (query_values.reshape(SLOTS, SEQ, QH * HD), key_values.reshape(SLOTS, SEQ, KVH * HD))


def draw_queries(key, part):
    return query_key_pair(key)[0].astype(jnp.bfloat16)


def draw_key_states(key, part):
    return query_key_pair(key)[1].astype(jnp.bfloat16)


def draw_layer_input(key, part):
    seeds = jax.random.split(jax.random.fold_in(key, 3301), 3)
    position_ramp = 0.6 * 3.0 ** (jnp.arange(SEQ, dtype=jnp.float32) / max(SEQ - 1, 1))
    feature_ramp = 0.6 * 3.0 ** (jnp.arange(D, dtype=jnp.float32) / (D - 1))
    row_scale = jnp.exp(jax.random.uniform(seeds[0], (SLOTS, SEQ, 1), jnp.float32, math.log(0.3), math.log(3.0)))
    row_scale = row_scale * position_ramp[None, :, None]
    column_scale = jnp.exp(jax.random.uniform(seeds[1], (SLOTS, 1, D), jnp.float32, math.log(0.3), math.log(3.0)))
    column_scale = column_scale * feature_ramp[None, None, :]
    base_values = jnp.clip(jax.random.normal(seeds[2], (SLOTS, SEQ, D), jnp.float32), -4.0, 4.0)
    return (base_values * row_scale * column_scale).astype(jnp.bfloat16)


def draw_out_grads(key, part):
    seeds = jax.random.split(jax.random.fold_in(key, 4401), 2)
    width = QH * HD
    column_scale = jnp.exp(jax.random.uniform(seeds[0], (SLOTS, 1, width), jnp.float32, math.log(0.3), math.log(3.0)))
    base_values = jnp.clip(jax.random.normal(seeds[1], (SLOTS, SEQ, width), jnp.float32), -4.0, 4.0)
    return (base_values * column_scale).astype(jnp.bfloat16)


def draw_lengths(key, part):
    seeds = jax.random.split(jax.random.fold_in(key, 5501), 3)
    base_values = jax.random.randint(seeds[0], (SLOTS,), SEQ // 8, SEQ + 1, dtype=jnp.int32)
    empty = jax.random.randint(seeds[1], (SLOTS,), 0, 4, dtype=jnp.int32) == 0
    base_values = jnp.where(empty, jnp.zeros_like(base_values), base_values)
    shuffled = jax.random.permutation(seeds[2], SLOTS)
    slot_index = jnp.arange(SLOTS, dtype=jnp.int32)
    base_values = jnp.where(slot_index == shuffled[0], SEQ, base_values)
    base_values = jnp.where(slot_index == shuffled[1], 0, base_values)
    return base_values.astype(jnp.int32)


def centred(key, extent, scale, bound, held_as=jnp.bfloat16):
    return jnp.clip(scale * jax.random.normal(key, extent, jnp.float32), -bound, bound).astype(held_as)


def setup_inputs(seed: int = 0) -> dict:
    keys = jax.random.split(jax.random.key(seed), 7)
    return {
        "layer_input": draw_layer_input(jax.random.fold_in(keys[6], 71), 0),
        "value_weight": centred(keys[1], (D, KVH * HD), D ** -0.5, 0.0625),
        "queries": draw_queries(jax.random.fold_in(keys[6], 71), 0),
        "key_states": draw_key_states(jax.random.fold_in(keys[6], 71), 0),
        "out_grads": draw_out_grads(jax.random.fold_in(keys[6], 71), 0),
        "lengths": draw_lengths(jax.random.fold_in(keys[6], 71), 0),
    }


def head_grads(query_rows, grad_rows, key_rows, value_rows, causal, softmax_scale):
    scores = jnp.dot(query_rows, key_rows.T, preferred_element_type=jnp.float32) * softmax_scale
    scores = jnp.where(causal, scores, -jnp.inf)
    row_peak = lax.optimization_barrier(jnp.max(scores, axis=-1, keepdims=True))
    weights = jnp.exp(scores - row_peak)
    weights = weights / lax.optimization_barrier(jnp.sum(weights, axis=-1, keepdims=True))
    probs_low = weights.astype(jnp.bfloat16)
    attended = jnp.dot(probs_low, value_rows, preferred_element_type=jnp.float32)
    offsets = lax.optimization_barrier(jnp.sum(grad_rows.astype(jnp.float32) * attended, axis=-1))
    grad_probs = jnp.dot(grad_rows, value_rows.T, preferred_element_type=jnp.float32)
    grad_scores = (weights * (grad_probs - offsets[:, None])).astype(jnp.bfloat16)
    key_part = jnp.dot(grad_scores.T, query_rows, preferred_element_type=jnp.float32) * softmax_scale
    value_part = jnp.dot(probs_low.T, grad_rows, preferred_element_type=jnp.float32)
    return (key_part, value_part)

def reference(layer_input, value_weight, queries, key_states, out_grads, lengths):
    softmax_scale = HD ** (-0.5)
    positions = jnp.arange(SEQ, dtype=jnp.int32)
    causal = positions[:, None] >= positions[None, :]
    clip_norm = math.sqrt(D * KVH * HD)

    def one_slot(running, slot_data):
        input_doc, query_doc, key_doc, grad_doc, length = slot_data
        value_doc = jnp.dot(input_doc, value_weight, preferred_element_type=jnp.float32).astype(jnp.bfloat16)
        grad_doc = jnp.where((positions < length)[:, None], grad_doc, jnp.zeros_like(grad_doc))
        query_heads = query_doc.reshape(SEQ, QH, HD).transpose(1, 0, 2)
        grad_heads = grad_doc.reshape(SEQ, QH, HD).transpose(1, 0, 2)
        key_heads = jnp.repeat(key_doc.reshape(SEQ, KVH, HD).transpose(1, 0, 2), QH // KVH, axis=0)
        value_heads = jnp.repeat(value_doc.reshape(SEQ, KVH, HD).transpose(1, 0, 2), QH // KVH, axis=0)

        def one_head(head_data):
            return head_grads(head_data[0], head_data[1], head_data[2], head_data[3], causal, softmax_scale)
        key_parts, value_parts = lax.map(one_head, (query_heads, grad_heads, key_heads, value_heads))
        key_sum = key_parts.reshape(KVH, QH // KVH, SEQ, HD).sum(axis=1).transpose(1, 0, 2).reshape(SEQ, KVH * HD)
        value_sum = value_parts.reshape(KVH, QH // KVH, SEQ, HD).sum(axis=1).transpose(1, 0, 2).reshape(SEQ, KVH * HD)
        value_low = value_sum.astype(jnp.bfloat16)
        doc_grad = jnp.dot(input_doc.T, value_low, preferred_element_type=jnp.float32)
        doc_norm = jnp.sqrt(jnp.sum(doc_grad * doc_grad))
        running = running + doc_grad * (clip_norm / (doc_norm + 0.01))
        return (running, (doc_norm, key_sum.astype(jnp.bfloat16)))
    running_sum = jnp.zeros((D, KVH * HD), jnp.float32)
    clipped_sum, (doc_norms, key_grads) = lax.scan(one_slot, running_sum, (layer_input, queries, key_states, out_grads, lengths))
    return (clipped_sum, doc_norms, key_grads)
```

```python
import functools
import math

import jax
import jax.numpy as jnp
from jax import lax
from jax.experimental import pallas as pl
from jax.experimental.pallas import tpu as pltpu
from jax.sharding import PartitionSpec as P

MESH = pl.DeviceIdType.MESH
BF = jnp.bfloat16
F32 = jnp.float32

D = 8192
HD = 128
KV = 512
NX = 4
NY = 4
NC = NX * NY
ND = 16
ROWS = 128
GH = 8
GW = GH * HD
SEQ = NC * ROWS
CK = NY * ROWS
KS = 256
STEPS = CK // KS
DB = D // NC
CB = KV // ND
WCH = 8
SCALE = HD ** (-0.5)
C2 = SCALE * math.log2(math.e)
CLIP = math.sqrt(D * KV)

K1, Q, G, K2, V1, V2, RV, RK, KO = range(0, 36, 4)
XT, AG, NM, GR, FC = range(36, 36 + 80, 16)
K2S, V2S, NSEM = 116, 128, 140
LX, LQ, LG, LK, LV, LXG, LW = 0, 1, 2, 3, 4, 5, 6


def attend(k, y, length, qb, gb, kf, vf, dk, dv, qs, gs, qt, gt, p_s, d_s, m_s):
    q_pos = CK * k + ROWS * y + lax.broadcasted_iota(jnp.int32, (ROWS, HD), 0)
    keep = q_pos < length
    for h in range(GH):
        cols = slice(h * HD, (h + 1) * HD)
        q = qb[k, :, cols]
        g = jnp.where(keep, gb[k, :, cols].astype(F32), 0.0)
        qs[cols, :] = q
        gs[cols, :] = g.astype(BF)
        qt[:, cols] = q.astype(F32).T.astype(BF)
        gt[:, cols] = g.T.astype(BF)

    def sweep_a(j, carry, masked):
        m, l, off = carry
        rows = pl.ds(pl.multiple_of(j * KS, KS), KS)
        s = jnp.dot(kf[rows, :], qt[...], preferred_element_type=F32)
        dp = jnp.dot(vf[rows, :], gt[...], preferred_element_type=F32)
        if masked:
            ki = lax.broadcasted_iota(jnp.int32, (KS, GW), 0)
            qi = lax.broadcasted_iota(jnp.int32, (KS, GW), 1) & (HD - 1)
            s = jnp.where(ki - qi <= CK * k + ROWS * y - KS * j, s, -jnp.inf)
        mn = jnp.maximum(m, jnp.max(s, axis=0, keepdims=True))
        a = jnp.exp2((m - mn) * C2)
        p = jnp.exp2((s - mn) * C2)
        p_s[rows, :] = p
        d_s[rows, :] = dp
        m_s[j] = jnp.broadcast_to(mn, (8, GW))
        l = l * a + jnp.sum(p, axis=0, keepdims=True)
        off = off * a + jnp.sum(p * dp, axis=0, keepdims=True)
        return mn, l, off

    zero = jnp.zeros((1, GW), F32)
    carry = (jnp.full((1, GW), -jnp.inf, F32), zero, zero)
    carry = lax.fori_loop(0, k * STEPS, lambda j, c: sweep_a(j, c, False), carry)
    for t in range(STEPS):
        carry = sweep_a(k * STEPS + t, carry, True)
    m, l, off = carry
    inv = 1.0 / l
    off = off * inv

    def sweep_b(j, _):
        rows = pl.ds(pl.multiple_of(j * KS, KS), KS)
        p = p_s[rows, :] * (jnp.exp2((m_s[j][0:1] - m) * C2) * inv)
        ds = p * (d_s[rows, :] - off)
        dv[rows, :] += jnp.dot(p.astype(BF), gs[...], preferred_element_type=F32)
        dk[rows, :] += jnp.dot(ds.astype(BF), qs[...], preferred_element_type=F32)
        return 0

    lax.fori_loop(0, (k + 1) * STEPS, sweep_b, 0)


def kernel(
    len_ref, x_ref, w_ref, q_ref, k_ref, g_ref,
    cs_ref, nm_ref, kg_ref,
    xv, wv, vown, qb, gb, kf, vf, xg, dk, dv, qs, gs, qt, gt, p_s, d_s, m_s,
    dvs, dks, dvr, dkr, kout, kin, dvt, acc, gsend, gr, nsend, nr, fsend, fr,
    send, recv, local,
):
    c = lax.axis_index("context")
    d = lax.axis_index("dp")
    x, y = c // NY, lax.rem(c, NY)
    length = len_ref[0]
    sent = []

    def at_x(o):
        return lax.rem(x + o, NX)

    def at_y(o):
        return lax.rem(y + o, NY)

    def remote(src, dst, sem, **peer):
        copy = pltpu.make_async_remote_copy(
            src_ref=src, dst_ref=dst, send_sem=send.at[sem], recv_sem=recv.at[sem],
            device_id=peer, device_id_type=MESH,
        )
        copy.start()
        sent.append(copy)
        return copy

    def near(src, dst, sem):
        copy = pltpu.make_async_copy(src, dst, local.at[sem])
        copy.start()
        return copy

    def cols(index, width):
        return pl.ds(pl.multiple_of(index * width, width), width)

    def place(ref, xi, yi):
        return ref.at[cols(xi * NY + yi, ROWS), :]

    load_x = near(x_ref, xv, LX)
    load_w = [near(w_ref.at[pl.ds(i * (D // WCH), D // WCH), :], wv.at[i], LW + i) for i in range(WCH)]
    own = [
        near(k_ref.at[:, cols(x, HD)], place(kf, x, y), LK),
        near(q_ref.at[:, cols(x, GW)], qb.at[x], LQ),
        near(g_ref.at[:, cols(x, GW)], gb.at[x], LG),
        near(x_ref.at[:, cols(c, DB)], xg.at[y, cols(x, ROWS), :], LXG),
    ]

    barrier = pltpu.get_barrier_semaphore()
    for i in range(NX):
        for j in range(NY):
            if i or j:
                peer = {"context": at_x(i) * NY + at_y(j)}
                pl.semaphore_signal(barrier, inc=1, device_id=peer, device_id_type=MESH)
    for o in range(1, ND):
        peer = {"dp": lax.rem(d + o, ND)}
        pl.semaphore_signal(barrier, inc=1, device_id=peer, device_id_type=MESH)
    pl.semaphore_wait(barrier, NC - 1 + ND - 1)

    k1 = [
        remote(k_ref.at[:, cols(at_x(o), HD)], place(kf, x, y), K1 + o, context=at_x(o) * NY + y)
        for o in range(1, NX)
    ]
    qc, gc = {}, {}
    for o in (1, 3, 2):
        there = at_x(o) * NY + y
        qc[o] = remote(q_ref.at[:, cols(at_x(o), GW)], qb.at[x], Q + o, context=there)
        gc[o] = remote(g_ref.at[:, cols(at_x(o), GW)], gb.at[x], G + o, context=there)

    def gather_y(ref, sem):
        copies = []
        for o in range(1, NY):
            for i in range(NX):
                copies.append(
                    remote(place(ref, i, y), place(ref, i, y), sem[o] + i, context=x * NY + at_y(o))
                )
        return copies

    own[0].wait()
    for copy in k1:
        copy.wait_recv()
    k2 = gather_y(kf, {o: K2S + 4 * (o - 1) for o in range(1, NY)})

    load_x.wait()
    total = jnp.zeros((ROWS, KV), F32)
    for i in range(WCH):
        load_w[i].wait()
        part = xv[:, i * (D // WCH) : (i + 1) * (D // WCH)]
        total += jnp.dot(part, wv[i], preferred_element_type=F32)
    vown[...] = total.astype(BF)
    v_own = near(vown.at[:, cols(x, HD)], place(vf, x, y), LV)
    v1 = [
        remote(vown.at[:, cols(at_x(o), HD)], place(vf, x, y), V1 + o, context=at_x(o) * NY + y)
        for o in range(1, NX)
    ]
    v_own.wait()
    for copy in v1:
        copy.wait_recv()
    v2 = gather_y(vf, {o: V2S + 4 * (o - 1) for o in range(1, NY)})

    xc = {}
    for i in range(NX):
        for j in range(NY):
            if i or j:
                there = at_x(i) * NY + at_y(j)
                dst = xg.at[y, cols(x, ROWS), :]
                xc[i, j] = remote(x_ref.at[:, cols(there, DB)], dst, XT + NY * i + j, context=there)

    dk[...] = jnp.zeros_like(dk)
    dv[...] = jnp.zeros_like(dv)
    for copy in k2 + v2:
        copy.wait_recv()
    for o in (0, 1, 3, 2):
        if o:
            qc[o].wait_recv()
            gc[o].wait_recv()
        else:
            own[1].wait()
            own[2].wait()
        k = lax.rem(x + NX - o, NX)
        attend(k, y, length, qb, gb, kf, vf, dk, dv, qs, gs, qt, gt, p_s, d_s, m_s)

    def split_y(ref, out, got, sem, scale):
        for yy in range(NY):
            for j in range(NX):
                block = ref[(j * NY + yy) * ROWS : (j * NY + yy + 1) * ROWS, :]
                out[yy, j] = (block * scale).astype(BF) if scale else block.astype(BF)
        return [
            remote(out.at[at_y(o)], got.at[o - 1], sem + o, context=x * NY + at_y(o))
            for o in range(1, NY)
        ]

    def summed(ref, got, j, scale):
        block = ref[cols(j * NY + y, ROWS), :]
        if scale:
            block = block * scale
        for o in range(1, NY):
            block = block + got[o - 1, j].astype(F32)
        return block

    rv = split_y(dv, dvs, dvr, RV, None)
    rk = split_y(dk, dks, dkr, RK, SCALE)
    for copy in rv:
        copy.wait_recv()
    for j in range(NX):
        dvt[y, cols(x, HD), j * ROWS : (j + 1) * ROWS] = summed(dv, dvr, j, None).T.astype(BF)
    ag = {}
    for i in range(NX):
        for j in range(NY):
            if i or j:
                part = dvt.at[y, cols(x, HD), :]
                there = at_x(i) * NY + at_y(j)
                ag[i, j] = remote(part, part, AG + NY * i + j, context=there)

    for copy in rk:
        copy.wait_recv()
    for j in range(NX):
        kout[j] = summed(dk, dkr, j, SCALE).astype(BF)
    kin[x] = kout[x]
    ko = [
        remote(kout.at[at_x(o)], kin.at[x], KO + o, context=at_x(o) * NY + y) for o in range(1, NX)
    ]

    own[3].wait()
    for j in range(NY):
        for i in range(NX):
            if i or j:
                xc[i, j].wait_recv()
                ag[i, j].wait_recv()
        yy = lax.rem(y + NY - j, NY)
        part = jnp.dot(dvt[yy], xg[yy], preferred_element_type=F32)
        acc[...] = part if j == 0 else acc[...] + part
    for i in range(ND):
        gsend[i] = acc[i * CB : (i + 1) * CB, :].astype(BF)
    gr[d] = gsend[d]
    gx = [
        remote(gsend.at[lax.rem(d + o, ND)], gr.at[d], GR + o, dp=lax.rem(d + o, ND))
        for o in range(1, ND)
    ]

    squares = jnp.sum(jnp.sum(acc[...] * acc[...], axis=0, keepdims=True), axis=1, keepdims=True)
    nsend[...] = jnp.broadcast_to(squares, (8, 128))
    nx = []
    for i in range(NX):
        for j in range(NY):
            if i or j:
                slot = NY * i + j
                there = at_x(i) * NY + at_y(j)
                nx.append(remote(nsend, nr.at[c], NM + slot, context=there))
    nr[c] = nsend[...]
    for copy in nx:
        copy.wait_recv()
    squares = nr[0]
    for i in range(1, NC):
        squares = squares + nr[i]
    norm = jnp.sqrt(squares)
    nm_ref[...] = norm
    fsend[...] = CLIP / (norm + 0.01)
    fx = [
        remote(fsend, fr.at[d], FC + o, dp=lax.rem(d + o, ND)) for o in range(1, ND)
    ]
    fr[d] = fsend[...]

    for copy in ko:
        copy.wait_recv()
    for i in range(NX):
        kg_ref[:, i * HD : (i + 1) * HD] = kin[i]

    for copy in fx + gx:
        copy.wait_recv()
    clipped = fr[0][0:1, 0:1] * gr[0].astype(F32)
    for i in range(1, ND):
        clipped = clipped + fr[i][0:1, 0:1] * gr[i].astype(F32)
    clipped = jnp.concatenate([clipped, jnp.zeros((128 - CB, DB), F32)], axis=0)
    cs_ref[...] = clipped.T[:, :CB]

    for copy in sent:
        copy.wait_send()


def body(layer_input, value_weight, queries, key_states, out_grads, lengths):
    vm = pltpu.VMEM
    anywhere = pl.BlockSpec(memory_space=pl.ANY)
    inside = pl.BlockSpec(memory_space=pltpu.VMEM)
    clipped, norm, key_grads = pl.pallas_call(
        kernel,
        out_shape=(
            jax.ShapeDtypeStruct((DB, CB), F32),
            jax.ShapeDtypeStruct((8, 128), F32),
            jax.ShapeDtypeStruct((ROWS, KV), BF),
        ),
        in_specs=[pl.BlockSpec(memory_space=pltpu.SMEM)] + [anywhere] * 5,
        out_specs=(inside, inside, inside),
        scratch_shapes=[
            vm((ROWS, D), BF),
            vm((WCH, D // WCH, KV), BF),
            vm((ROWS, KV), BF),
            vm((NX, ROWS, GW), BF),
            vm((NX, ROWS, GW), BF),
            vm((SEQ, HD), BF),
            vm((SEQ, HD), BF),
            vm((NY, CK, DB), BF),
            vm((SEQ, HD), F32),
            vm((SEQ, HD), F32),
            vm((GW, HD), BF),
            vm((GW, HD), BF),
            vm((HD, GW), BF),
            vm((HD, GW), BF),
            vm((SEQ, GW), F32),
            vm((SEQ, GW), F32),
            vm((SEQ // KS, 8, GW), F32),
            vm((NY, NX, ROWS, HD), BF),
            vm((NY, NX, ROWS, HD), BF),
            vm((NY - 1, NX, ROWS, HD), BF),
            vm((NY - 1, NX, ROWS, HD), BF),
            vm((NX, ROWS, HD), BF),
            vm((NX, ROWS, HD), BF),
            vm((NY, KV, CK), BF),
            vm((KV, DB), F32),
            vm((ND, CB, DB), BF),
            vm((ND, CB, DB), BF),
            vm((8, 128), F32),
            vm((NC, 8, 128), F32),
            vm((8, 128), F32),
            vm((ND, 8, 128), F32),
            pltpu.SemaphoreType.DMA((NSEM,)),
            pltpu.SemaphoreType.DMA((NSEM,)),
            pltpu.SemaphoreType.DMA((LW + WCH,)),
        ],
        compiler_params=pltpu.CompilerParams(
            collective_id=0, has_side_effects=True, vmem_limit_bytes=56 * 2**20
        ),
    )(lengths, layer_input[0], value_weight, queries[0], key_states[0], out_grads[0])
    return clipped, norm[0, 0:1], key_grads[None]


def solution(mesh):
    placed = (
        P("dp", "context", None),
        P(),
        P("dp", "context", None),
        P("dp", "context", None),
        P("dp", "context", None),
        P("dp"),
    )
    return jax.shard_map(
        body,
        mesh=mesh,
        in_specs=placed,
        out_specs=(P("context", "dp"), P("dp"), P("dp", "context", None)),
        check_vma=False,
    )
```

```python
import functools
import math

import jax
import jax.numpy as jnp
from jax import lax
from jax.experimental import pallas as pl
from jax.experimental.pallas import tpu as pltpu
from jax.sharding import PartitionSpec as P

MESH = pl.DeviceIdType.MESH
BF = jnp.bfloat16
F32 = jnp.float32

D = 8192
HD = 128
KV = 512
NX = 4
NY = 4
NC = NX * NY
ND = 16
ROWS = 128
GH = 8
GW = GH * HD
SEQ = NC * ROWS
CK = NY * ROWS
KS = 512
STEPS = CK // KS
DB = D // NC
CB = KV // ND
WCH = 8
SCALE = HD ** (-0.5)
C2 = SCALE * math.log2(math.e)
CLIP = math.sqrt(D * KV)

K1, Q, G, V1, RV, RK, KO, AX, AY, NA, NB = range(0, 44, 4)
K2, V2, XY, XX, AXF, AYF, GR, FC = range(44, 44 + 128, 16)
NSEM = 172
LX, LQ, LG, LK, LV, LXG, LW = 0, 1, 2, 3, 4, 5, 9


def attend(k, y, length, qb, gb, kf, vf, dk, dv, qs, gs, qt, gt, p_s, d_s, m_s):
    q_pos = CK * k + ROWS * y + lax.broadcasted_iota(jnp.int32, (ROWS, HD), 0)
    keep = q_pos < length
    for h in range(GH):
        cols = slice(h * HD, (h + 1) * HD)
        q = qb[k, :, cols]
        g = jnp.where(keep, gb[k, :, cols].astype(F32), 0.0)
        qs[cols, :] = q
        gs[cols, :] = g.astype(BF)
        qt[:, cols] = q.astype(F32).T.astype(BF)
        gt[:, cols] = g.T.astype(BF)

    def sweep_a(j, carry, masked):
        m, l, off = carry
        rows = pl.ds(pl.multiple_of(j * KS, KS), KS)
        s = jnp.dot(kf[rows, :], qt[...], preferred_element_type=F32)
        dp = jnp.dot(vf[rows, :], gt[...], preferred_element_type=F32)
        if masked:
            ki = lax.broadcasted_iota(jnp.int32, (KS, GW), 0)
            qi = lax.broadcasted_iota(jnp.int32, (KS, GW), 1) & (HD - 1)
            s = jnp.where(ki - qi <= CK * k + ROWS * y - KS * j, s, -jnp.inf)
        mn = jnp.maximum(m, jnp.max(s, axis=0, keepdims=True))
        a = jnp.exp2((m - mn) * C2)
        p = jnp.exp2((s - mn) * C2)
        p_s[rows, :] = p
        d_s[rows, :] = dp
        m_s[j] = jnp.broadcast_to(mn, (8, GW))
        l = l * a + jnp.sum(p, axis=0, keepdims=True)
        off = off * a + jnp.sum(p * dp, axis=0, keepdims=True)
        return mn, l, off

    zero = jnp.zeros((1, GW), F32)
    carry = (jnp.full((1, GW), -jnp.inf, F32), zero, zero)
    carry = lax.fori_loop(0, k * STEPS, lambda j, c: sweep_a(j, c, False), carry)
    for t in range(STEPS):
        carry = sweep_a(k * STEPS + t, carry, True)
    m, l, off = carry
    inv = 1.0 / l
    off = off * inv

    def sweep_b(j, _):
        rows = pl.ds(pl.multiple_of(j * KS, KS), KS)
        p = p_s[rows, :] * (jnp.exp2((m_s[j][0:1] - m) * C2) * inv)
        ds = p * (d_s[rows, :] - off)
        dv[rows, :] += jnp.dot(p.astype(BF), gs[...], preferred_element_type=F32)
        dk[rows, :] += jnp.dot(ds.astype(BF), qs[...], preferred_element_type=F32)
        return 0

    lax.fori_loop(0, (k + 1) * STEPS, sweep_b, 0)


def kernel(
    len_ref, x_ref, w_ref, q_ref, k_ref, g_ref,
    cs_ref, nm_ref, kg_ref,
    xv, wv, vown, qb, gb, kf, vf, xg, xs, dk, dv, qs, gs, qt, gt, p_s, d_s, m_s,
    dvs, dks, dvr, dkr, kout, kin, dvt, acc, gsend, gr, nsend, nr, fsend, fr,
    send, recv, local,
):
    c = lax.axis_index("context")
    d = lax.axis_index("dp")
    x, y = c // NY, lax.rem(c, NY)
    length = len_ref[0]
    sent = []

    def at_x(o):
        return lax.rem(x + o, NX)

    def at_y(o):
        return lax.rem(y + o, NY)

    def remote(src, dst, sem, **peer):
        copy = pltpu.make_async_remote_copy(
            src_ref=src, dst_ref=dst, send_sem=send.at[sem], recv_sem=recv.at[sem],
            device_id=peer, device_id_type=MESH,
        )
        copy.start()
        sent.append(copy)
        return copy

    def near(src, dst, sem):
        copy = pltpu.make_async_copy(src, dst, local.at[sem])
        copy.start()
        return copy

    def cols(index, width):
        return pl.ds(pl.multiple_of(index * width, width), width)

    def place(ref, xi, yi):
        return ref.at[cols(xi * NY + yi, ROWS), :]

    load_x = near(x_ref, xv, LX)
    load_w = [near(w_ref.at[pl.ds(i * (D // WCH), D // WCH), :], wv.at[i], LW + i) for i in range(WCH)]
    own = [
        near(k_ref.at[:, cols(x, HD)], place(kf, x, y), LK),
        near(q_ref.at[:, cols(x, GW)], qb.at[x], LQ),
        near(g_ref.at[:, cols(x, GW)], gb.at[x], LG),
    ]

    def staged(i, yi):
        return xs.at[i - 1, yi] if i else xg.at[yi, x]

    for i in range(NX):
        own.append(near(x_ref.at[:, cols(at_x(i) * NY + y, DB)], staged(i, y), LXG + i))

    def on_x(o):
        return {"context": at_x(o) * NY + y}

    def on_y(o):
        return {"context": x * NY + at_y(o)}

    def on_dp(o):
        return {"dp": lax.rem(d + o, ND)}

    barrier = pltpu.get_barrier_semaphore()
    peers = [on_x(o) for o in range(1, NX)] + [on_y(o) for o in range(1, NY)]
    peers += [on_dp(o) for o in range(1, ND)]
    for peer in peers:
        pl.semaphore_signal(barrier, inc=1, device_id=peer, device_id_type=MESH)
    pl.semaphore_wait(barrier, len(peers))

    k1 = [
        remote(k_ref.at[:, cols(at_x(o), HD)], place(kf, x, y), K1 + o, **on_x(o))
        for o in range(1, NX)
    ]
    qc, gc = {}, {}


    def queries_x(o):
        qc[o] = remote(q_ref.at[:, cols(at_x(o), GW)], qb.at[x], Q + o, **on_x(o))

    def grads_x(o):
        gc[o] = remote(g_ref.at[:, cols(at_x(o), GW)], gb.at[x], G + o, **on_x(o))

    queries_x(1)
    queries_x(3)

    def gather_y(ref, sem):
        copies = []
        for o in range(1, NY):
            for i in range(NX):
                copies.append(
                    remote(place(ref, i, y), place(ref, i, y), sem + NX * o + i, **on_y(o))
                )
        return copies

    own[0].wait()
    for copy in k1:
        copy.wait_recv()
    k2 = gather_y(kf, K2)

    load_x.wait()
    total = jnp.zeros((ROWS, KV), F32)
    for i in range(WCH):
        load_w[i].wait()
        part = xv[:, i * (D // WCH) : (i + 1) * (D // WCH)]
        total += jnp.dot(part, wv[i], preferred_element_type=F32)
    vown[...] = total.astype(BF)
    v_own = near(vown.at[:, cols(x, HD)], place(vf, x, y), LV)
    v1 = [
        remote(vown.at[:, cols(at_x(o), HD)], place(vf, x, y), V1 + o, **on_x(o))
        for o in range(1, NX)
    ]
    grads_x(1)
    grads_x(3)
    queries_x(2)
    grads_x(2)
    v_own.wait()
    for copy in v1:
        copy.wait_recv()
    v2 = gather_y(vf, V2)

    xy, xx = {}, {}

    def input_y(i):
        for o in range(1, NY):
            there = at_x(i) * NY + at_y(o)
            xy[i, o] = remote(
                x_ref.at[:, cols(there, DB)], staged(i, y), XY + NX * o + i, **on_y(o)
            )

    def input_x(i):
        own[3 + i].wait()
        for o in range(1, NY):
            xy[i, o].wait_recv()
        if i:
            xx[i] = remote(xs.at[i - 1], xg.at[:, x], XX + i, **on_x(i))

    input_y(1)
    input_y(3)
    dk[...] = jnp.zeros_like(dk)
    dv[...] = jnp.zeros_like(dv)
    for copy in k2 + v2:
        copy.wait_recv()
    input_y(2)
    input_y(0)
    for o in (0, 1, 3, 2):
        if o:
            qc[o].wait_recv()
            gc[o].wait_recv()
        else:
            own[1].wait()
            own[2].wait()
        k = lax.rem(x + NX - o, NX)
        attend(k, y, length, qb, gb, kf, vf, dk, dv, qs, gs, qt, gt, p_s, d_s, m_s)
        if o == 1:
            input_x(1)
            input_x(3)
        elif o == 3:
            input_x(2)

    def split_y(ref, out, got, sem, scale):
        for yy in range(NY):
            for j in range(NX):
                block = ref[(j * NY + yy) * ROWS : (j * NY + yy + 1) * ROWS, :]
                out[yy, j] = (block * scale).astype(BF) if scale else block.astype(BF)
        return [
            remote(out.at[at_y(o)], got.at[o - 1], sem + o, **on_y(o))
            for o in range(1, NY)
        ]

    def summed(ref, got, j, scale):
        block = ref[cols(j * NY + y, ROWS), :]
        if scale:
            block = block * scale
        for o in range(1, NY):
            block = block + got[o - 1, j].astype(F32)
        return block

    rv = split_y(dv, dvs, dvr, RV, None)
    for copy in rv:
        copy.wait_recv()
    for j in range(NX):
        dvt[y, cols(x, HD), j * ROWS : (j + 1) * ROWS] = summed(dv, dvr, j, None).T.astype(BF)
    half = CK // 2
    part = dvt.at[y, cols(x, HD), :]
    ax, ay, axf, ayf = {}, {}, {}, {}
    for o in (1, 3, 2):
        ax[o] = remote(part, part, AX + o, **on_x(o))
        ay[o] = remote(part, part, AY + o, **on_y(o))
    for o in (1, 3, 2):
        ax[o].wait_recv()
        part = dvt.at[y, cols(lax.rem(x + NX - o, NX), HD), half:]
        for j in (1, 3, 2):
            ayf[o, j] = remote(part, part, AYF + NY * o + j, **on_y(j))
        ay[o].wait_recv()
        part = dvt.at[lax.rem(y + NY - o, NY), cols(x, HD), :half]
        for i in (1, 3, 2):
            axf[i, o] = remote(part, part, AXF + NY * i + o, **on_x(i))
    rk = split_y(dk, dks, dkr, RK, SCALE)

    input_x(0)
    for i in range(1, NX):
        xx[i].wait_recv()
    for j in range(NY):
        for i in range(1, NX):
            if j:
                axf[i, j].wait_recv()
                ayf[i, j].wait_recv()
        yy = lax.rem(y + NY - j, NY)
        part = jnp.dot(dvt[yy], xg[yy].reshape(CK, DB), preferred_element_type=F32)
        acc[...] = part if j == 0 else acc[...] + part
    for i in range(ND):
        gsend[i] = acc[i * CB : (i + 1) * CB, :].astype(BF)
    gr[d] = gsend[d]
    gx = [
        remote(gsend.at[lax.rem(d + o, ND)], gr.at[d], GR + o, **on_dp(o))
        for o in range(1, ND)
    ]

    squares = jnp.sum(jnp.sum(acc[...] * acc[...], axis=0, keepdims=True), axis=1, keepdims=True)
    squares = jnp.broadcast_to(squares, (8, 128))
    for step, (on, sem) in enumerate(((on_x, NA), (on_y, NB))):
        mine = y if step else x
        nsend[step] = squares
        copies = [remote(nsend.at[step], nr.at[step, mine], sem + o, **on(o)) for o in range(1, NX)]
        nr[step, mine] = squares
        for copy in copies:
            copy.wait_recv()
        squares = (nr[step, 0] + nr[step, 1]) + (nr[step, 2] + nr[step, 3])
    norm = jnp.sqrt(squares)
    nm_ref[...] = norm
    fsend[...] = CLIP / (norm + 0.01)
    fx = [
        remote(fsend, fr.at[d], FC + o, **on_dp(o)) for o in range(1, ND)
    ]
    fr[d] = fsend[...]

    for copy in rk:
        copy.wait_recv()
    for j in range(NX):
        kout[j] = summed(dk, dkr, j, SCALE).astype(BF)
    kin[x] = kout[x]
    ko = [
        remote(kout.at[at_x(o)], kin.at[x], KO + o, **on_x(o)) for o in range(1, NX)
    ]
    for copy in ko:
        copy.wait_recv()
    for i in range(NX):
        kg_ref[:, i * HD : (i + 1) * HD] = kin[i]

    for copy in fx + gx:
        copy.wait_recv()
    clipped = fr[0][0:1, 0:1] * gr[0].astype(F32)
    for i in range(1, ND):
        clipped = clipped + fr[i][0:1, 0:1] * gr[i].astype(F32)
    clipped = jnp.concatenate([clipped, jnp.zeros((128 - CB, DB), F32)], axis=0)
    cs_ref[...] = clipped.T[:, :CB]

    for copy in sent:
        copy.wait_send()


def body(layer_input, value_weight, queries, key_states, out_grads, lengths):
    vm = pltpu.VMEM
    anywhere = pl.BlockSpec(memory_space=pl.ANY)
    inside = pl.BlockSpec(memory_space=pltpu.VMEM)
    clipped, norm, key_grads = pl.pallas_call(
        kernel,
        out_shape=(
            jax.ShapeDtypeStruct((DB, CB), F32),
            jax.ShapeDtypeStruct((8, 128), F32),
            jax.ShapeDtypeStruct((ROWS, KV), BF),
        ),
        in_specs=[pl.BlockSpec(memory_space=pltpu.SMEM)] + [anywhere] * 5,
        out_specs=(inside, inside, inside),
        scratch_shapes=[
            vm((ROWS, D), BF),
            vm((WCH, D // WCH, KV), BF),
            vm((ROWS, KV), BF),
            vm((NX, ROWS, GW), BF),
            vm((NX, ROWS, GW), BF),
            vm((SEQ, HD), BF),
            vm((SEQ, HD), BF),
            vm((NY, NX, ROWS, DB), BF),
            vm((NX - 1, NY, ROWS, DB), BF),
            vm((SEQ, HD), F32),
            vm((SEQ, HD), F32),
            vm((GW, HD), BF),
            vm((GW, HD), BF),
            vm((HD, GW), BF),
            vm((HD, GW), BF),
            vm((SEQ, GW), F32),
            vm((SEQ, GW), F32),
            vm((SEQ // KS, 8, GW), F32),
            vm((NY, NX, ROWS, HD), BF),
            vm((NY, NX, ROWS, HD), BF),
            vm((NY - 1, NX, ROWS, HD), BF),
            vm((NY - 1, NX, ROWS, HD), BF),
            vm((NX, ROWS, HD), BF),
            vm((NX, ROWS, HD), BF),
            vm((NY, KV, CK), BF),
            vm((KV, DB), F32),
            vm((ND, CB, DB), BF),
            vm((ND, CB, DB), BF),
            vm((2, 8, 128), F32),
            vm((2, NX, 8, 128), F32),
            vm((8, 128), F32),
            vm((ND, 8, 128), F32),
            pltpu.SemaphoreType.DMA((NSEM,)),
            pltpu.SemaphoreType.DMA((NSEM,)),
            pltpu.SemaphoreType.DMA((LW + WCH,)),
        ],
        compiler_params=pltpu.CompilerParams(
            collective_id=0, has_side_effects=True, vmem_limit_bytes=56 * 2**20
        ),
    )(lengths, layer_input[0], value_weight, queries[0], key_states[0], out_grads[0])
    return clipped, norm[0, 0:1], key_grads[None]


def solution(mesh):
    placed = (
        P("dp", "context", None),
        P(),
        P("dp", "context", None),
        P("dp", "context", None),
        P("dp", "context", None),
        P("dp"),
    )
    return jax.shard_map(
        body,
        mesh=mesh,
        in_specs=placed,
        out_specs=(P("context", "dp"), P("dp"), P("dp", "context", None)),
        check_vma=False,
    )
```

```python
import functools
import math

import jax
import jax.numpy as jnp
from jax import lax
from jax.experimental import pallas as pl
from jax.experimental.pallas import tpu as pltpu
from jax.sharding import PartitionSpec as P

MESH = pl.DeviceIdType.MESH
BF = jnp.bfloat16
F32 = jnp.float32

D = 8192
HD = 128
KV = 512
NX = 4
NY = 4
NC = NX * NY
ND = 16
ROWS = 128
GH = 8
GW = GH * HD
SEQ = NC * ROWS
CK = NY * ROWS
KS = 512
STEPS = CK // KS
DB = D // NC
DH = DB // 2
CB = KV // ND
WCH = 8
SCALE = HD ** (-0.5)
C2 = SCALE * math.log2(math.e)
CLIP = math.sqrt(D * KV)

K1, Q, G, V1, RK, KO, AX, AY = range(0, 32, 4)
K2, V2, XY, XX, AXF, AYF, GR, FC, RV, NM = range(32, 32 + 10 * 32, 32)
NSEM = 352
LX, LQ, LG, LK, LV, LXG, LW = 0, 1, 2, 3, 4, 5, 13

def attend(k, y, length, qb, gb, kf, vf, dk, dv, qs, gs, qt, gt, p_s, d_s, m_s, done):
    q_pos = CK * k + ROWS * y + lax.broadcasted_iota(jnp.int32, (ROWS, HD), 0)
    keep = q_pos < length
    for h in range(GH):
        cols = slice(h * HD, (h + 1) * HD)
        q = qb[k, :, cols]
        g = jnp.where(keep, gb[k, :, cols].astype(F32), 0.0)
        qs[cols, :] = q
        gs[cols, :] = g.astype(BF)
        qt[:, cols] = q.astype(F32).T.astype(BF)
        gt[:, cols] = g.T.astype(BF)

    def sweep_a(j, carry, masked):
        m, l, off = carry
        rows = pl.ds(pl.multiple_of(j * KS, KS), KS)
        s = jnp.dot(kf[rows, :], qt[...], preferred_element_type=F32)
        dp = jnp.dot(vf[rows, :], gt[...], preferred_element_type=F32)
        if masked:
            ki = lax.broadcasted_iota(jnp.int32, (KS, GW), 0)
            qi = lax.broadcasted_iota(jnp.int32, (KS, GW), 1) & (HD - 1)
            s = jnp.where(ki - qi <= CK * k + ROWS * y - KS * j, s, -jnp.inf)
        mn = jnp.maximum(m, jnp.max(s, axis=0, keepdims=True))
        a = jnp.exp2((m - mn) * C2)
        p = jnp.exp2((s - mn) * C2)
        p_s[rows, :] = p
        d_s[rows, :] = dp
        m_s[j] = jnp.broadcast_to(mn, (8, GW))
        l = l * a + jnp.sum(p, axis=0, keepdims=True)
        off = off * a + jnp.sum(p * dp, axis=0, keepdims=True)
        return mn, l, off

    zero = jnp.zeros((1, GW), F32)
    carry = (jnp.full((1, GW), -jnp.inf, F32), zero, zero)
    carry = lax.fori_loop(0, k * STEPS, lambda j, c: sweep_a(j, c, False), carry)
    for t in range(STEPS):
        carry = sweep_a(k * STEPS + t, carry, True)
    m, l, off = carry
    inv = 1.0 / l
    off = off * inv

    def sweep_b(j, _):
        rows = pl.ds(pl.multiple_of(j * KS, KS), KS)
        p = p_s[rows, :] * (jnp.exp2((m_s[j][0:1] - m) * C2) * inv)
        ds = p * (d_s[rows, :] - off)
        dv[rows, :] += jnp.dot(p.astype(BF), gs[...], preferred_element_type=F32)
        dk[rows, :] += jnp.dot(ds.astype(BF), qs[...], preferred_element_type=F32)
        if done:
            done(j)
        return 0

    lax.fori_loop(0, (k + 1) * STEPS, sweep_b, 0)

def kernel(
    len_ref, x_ref, w_ref, q_ref, k_ref, g_ref,
    cs_ref, nm_ref, kg_ref,
    xv, wv, vown, qb, gb, kf, vf, xg, xs, dk, dv, qs, gs, qt, gt, p_s, d_s, m_s,
    dvs, dks, dvr, dkr, kout, kin, dvt, acc, gsend, gr, nsend, nr, fsend, fr,
    send, recv, local,
):
    c = lax.axis_index("context")
    d = lax.axis_index("dp")
    x, y = c // NY, lax.rem(c, NY)
    length = len_ref[0]
    sent = []

    def at_x(o):
        return lax.rem(x + o, NX)

    def at_y(o):
        return lax.rem(y + o, NY)

    def remote(src, dst, sem, **peer):
        copy = pltpu.make_async_remote_copy(
            src_ref=src, dst_ref=dst, send_sem=send.at[sem], recv_sem=recv.at[sem],
            device_id=peer, device_id_type=MESH,
        )
        copy.start()
        sent.append(copy)
        return copy

    def near(src, dst, sem):
        copy = pltpu.make_async_copy(src, dst, local.at[sem])
        copy.start()
        return copy

    def cols(index, width):
        return pl.ds(pl.multiple_of(index * width, width), width)

    def place(ref, xi, yi):
        return ref.at[cols(xi * NY + yi, ROWS), :]

    load_x = near(x_ref, xv, LX)
    load_w = [near(w_ref.at[pl.ds(i * (D // WCH), D // WCH), :], wv.at[i], LW + i) for i in range(WCH)]
    own = [
        near(k_ref.at[:, cols(x, HD)], place(kf, x, y), LK),
        near(q_ref.at[:, cols(x, GW)], qb.at[x], LQ),
        near(g_ref.at[:, cols(x, GW)], gb.at[x], LG),
    ]

    def staged(h, i, yi):
        return xs.at[h, i - 1, yi] if i else xg.at[h, yi, x]

    def input_cols(h, there):
        return x_ref.at[:, pl.ds(pl.multiple_of(there * DB + h * DH, DH), DH)]

    for h in range(2):
        for i in range(NX):
            src = input_cols(h, at_x(i) * NY + y)
            own.append(near(src, staged(h, i, y), LXG + NX * h + i))

    def on_x(o):
        return {"context": at_x(o) * NY + y}

    def on_y(o):
        return {"context": x * NY + at_y(o)}

    def on_dp(o):
        return {"dp": lax.rem(d + o, ND)}

    def on_xy(i, j):
        return {"context": at_x(i) * NY + at_y(j)}

    barrier = pltpu.get_barrier_semaphore()
    others = [(i, j) for i in range(NX) for j in range(NY) if i or j]
    peers = [on_xy(i, j) for i, j in others] + [on_dp(o) for o in range(1, ND)]
    for peer in peers:
        pl.semaphore_signal(barrier, inc=1, device_id=peer, device_id_type=MESH)

    dk[...] = jnp.zeros_like(dk)
    dv[...] = jnp.zeros_like(dv)
    load_x.wait()
    total = jnp.zeros((ROWS, KV), F32)
    for i in range(WCH):
        load_w[i].wait()
        part = xv[:, i * (D // WCH) : (i + 1) * (D // WCH)]
        total += jnp.dot(part, wv[i], preferred_element_type=F32)
    vown[...] = total.astype(BF)
    v_own = near(vown.at[:, cols(x, HD)], place(vf, x, y), LV)

    pl.semaphore_wait(barrier, len(peers))

    v1 = [
        remote(vown.at[:, cols(at_x(o), HD)], place(vf, x, y), V1 + o, **on_x(o))
        for o in range(1, NX)
    ]
    k1 = [
        remote(k_ref.at[:, cols(at_x(o), HD)], place(kf, x, y), K1 + o, **on_x(o))
        for o in range(1, NX)
    ]
    qc, gc = {}, {}

    def queries_x(o):
        qc[o] = remote(q_ref.at[:, cols(at_x(o), GW)], qb.at[x], Q + o, **on_x(o))

    def grads_x(o):
        gc[o] = remote(g_ref.at[:, cols(at_x(o), GW)], gb.at[x], G + o, **on_x(o))

    for o in (1, 3, 2):
        queries_x(o)
        grads_x(o)

    def gather_y(ref, sem):
        copies = []
        for o in range(1, NY):
            for i in range(NX):
                copies.append(
                    remote(place(ref, i, y), place(ref, i, y), sem + NX * o + i, **on_y(o))
                )
        return copies

    own[0].wait()
    for copy in k1:
        copy.wait_recv()
    k2 = gather_y(kf, K2)

    v_own.wait()
    for copy in v1:
        copy.wait_recv()
    v2 = gather_y(vf, V2)

    xy, xx = {}, {}

    def input_y(h, i):
        for o in range(1, NY):
            src = input_cols(h, at_x(i) * NY + at_y(o))
            sem = XY + NC * h + NX * o + i
            xy[h, i, o] = remote(src, staged(h, i, y), sem, **on_y(o))

    def input_x(h, i):
        own[3 + NX * h + i].wait()
        for o in range(1, NY):
            xy[h, i, o].wait_recv()
        if i:
            xx[h, i] = remote(xs.at[h, i - 1], xg.at[h, :, x], XX + NX * h + i, **on_x(i))

    for i in (1, 3, 2, 0):
        input_y(0, i)
    for copy in k2 + v2:
        copy.wait_recv()
    for i in (1, 3, 2, 0):
        input_y(1, i)
    def sum_copy(o, j):
        sem = RV + NX * o + j
        return pltpu.make_async_remote_copy(
            src_ref=dvs.at[at_y(o), j], dst_ref=dvr.at[o - 1, j], send_sem=send.at[sem],
            recv_sem=recv.at[sem], device_id=on_y(o), device_id_type=MESH,
        )

    def sum_start(j):
        for yy in range(NY):
            dvs[yy, j] = dv[cols(j * NY + yy, ROWS), :].astype(BF)
        for o in range(1, NY):
            sum_copy(o, j).start()
        return 0

    for o in (0, 1, 3, 2):
        if o:
            qc[o].wait_recv()
            gc[o].wait_recv()
        else:
            own[1].wait()
            own[2].wait()
        k = lax.rem(x + NX - o, NX)
        done = None
        if o == 2:
            done = sum_start
            lax.fori_loop(k + 1, NX, lambda j, _: sum_start(j), 0)
        attend(k, y, length, qb, gb, kf, vf, dk, dv, qs, gs, qt, gt, p_s, d_s, m_s, done)
        if o == 1:
            input_x(0, 1)
            input_x(0, 3)
        elif o == 3:
            input_x(0, 2)

    def split_y(ref, out, got, sem, scale):
        for yy in range(NY):
            for j in range(NX):
                block = ref[(j * NY + yy) * ROWS : (j * NY + yy + 1) * ROWS, :]
                out[yy, j] = (block * scale).astype(BF) if scale else block.astype(BF)
        return [
            remote(out.at[at_y(o)], got.at[o - 1], sem + o, **on_y(o))
            for o in range(1, NY)
        ]

    def summed(ref, got, j, scale):
        block = ref[cols(j * NY + y, ROWS), :]
        if scale:
            block = block * scale
        for o in range(1, NY):
            block = block + got[o - 1, j].astype(F32)
        return block

    rv = [sum_copy(o, j) for j in range(NX) for o in range(1, NY)]
    sent.extend(rv)
    input_x(1, 1)
    input_x(1, 3)
    for copy in rv:
        copy.wait_recv()
    for j in range(NX):
        dvt[y, cols(x, HD), j * ROWS : (j + 1) * ROWS] = summed(dv, dvr, j, None).T.astype(BF)
    half = CK // 2
    part = dvt.at[y, cols(x, HD), :]
    ax, ay, axf, ayf = {}, {}, {}, {}
    for o in (1, 3, 2):
        ax[o] = remote(part, part, AX + o, **on_x(o))
        ay[o] = remote(part, part, AY + o, **on_y(o))
    for o in (1, 3, 2):
        ax[o].wait_recv()
        part = dvt.at[y, cols(lax.rem(x + NX - o, NX), HD), half:]
        for j in (1, 3, 2):
            ayf[o, j] = remote(part, part, AYF + NY * o + j, **on_y(j))
        ay[o].wait_recv()
        part = dvt.at[lax.rem(y + NY - o, NY), cols(x, HD), :half]
        for i in (1, 3, 2):
            axf[i, o] = remote(part, part, AXF + NY * i + o, **on_x(i))
    input_x(1, 2)
    rk = split_y(dk, dks, dkr, RK, SCALE)

    squares = jnp.zeros((1, 1), F32)
    gx = []
    for h in range(2):
        input_x(h, 0)
        for i in range(1, NX):
            xx[h, i].wait_recv()
        for j in (0, 1, 3, 2):
            if h == 0:
                for i in range(1, NX):
                    if j:
                        axf[i, j].wait_recv()
                        ayf[i, j].wait_recv()
            yy = lax.rem(y + NY - j, NY)
            part = jnp.dot(dvt[yy], xg[h, yy].reshape(CK, DH), preferred_element_type=F32)
            acc[...] = acc[...] + part if j else part
        total = acc[...]
        for i in range(ND):
            gsend[h, i] = total[i * CB : (i + 1) * CB, :].astype(BF)
        gr[h, d] = gsend[h, d]
        for o in range(1, ND):
            there = lax.rem(d + o, ND)
            gx.append(remote(gsend.at[h, there], gr.at[h, d], GR + ND * h + o, **on_dp(o)))
        columns = jnp.sum(total * total, axis=0, keepdims=True)
        squares = squares + jnp.sum(columns, axis=1, keepdims=True)
    nsend[...] = jnp.broadcast_to(squares, (8, 128))
    nx = [remote(nsend, nr.at[c], NM + NY * i + j, **on_xy(i, j)) for i, j in others]
    nr[c] = nsend[...]
    for copy in nx:
        copy.wait_recv()
    squares = nr[0]
    for i in range(1, NC):
        squares = squares + nr[i]
    norm = jnp.sqrt(squares)
    nm_ref[...] = norm
    fsend[...] = CLIP / (norm + 0.01)
    fx = [
        remote(fsend, fr.at[d], FC + o, **on_dp(o)) for o in range(1, ND)
    ]
    fr[d] = fsend[...]

    for copy in rk:
        copy.wait_recv()
    for j in range(NX):
        kout[j] = summed(dk, dkr, j, SCALE).astype(BF)
    kin[x] = kout[x]
    ko = [
        remote(kout.at[at_x(o)], kin.at[x], KO + o, **on_x(o)) for o in range(1, NX)
    ]
    for copy in ko:
        copy.wait_recv()
    for i in range(NX):
        kg_ref[:, i * HD : (i + 1) * HD] = kin[i]

    for copy in fx + gx:
        copy.wait_recv()
    for h in range(2):
        clipped = fr[0][0:1, 0:1] * gr[h, 0].astype(F32)
        for i in range(1, ND):
            clipped = clipped + fr[i][0:1, 0:1] * gr[h, i].astype(F32)
        cs_ref[:, h * DH : (h + 1) * DH] = clipped

    for copy in sent:
        copy.wait_send()

def finish(clipped_ref, norm_ref, key_ref, cs_ref, nm_ref, kg_ref):
    cs_ref[...] = clipped_ref[...]
    nm_ref[0] = norm_ref[0, 0]
    kg_ref[0] = key_ref[...]

def body(layer_input, value_weight, queries, key_states, out_grads, lengths):
    vm = pltpu.VMEM
    anywhere = pl.BlockSpec(memory_space=pl.ANY)
    inside = pl.BlockSpec(memory_space=pltpu.VMEM)
    clipped, norm, key_grads = pl.pallas_call(
        kernel,
        out_shape=(
            jax.ShapeDtypeStruct((CB, DB), F32),
            jax.ShapeDtypeStruct((8, 128), F32),
            jax.ShapeDtypeStruct((ROWS, KV), BF),
        ),
        in_specs=[pl.BlockSpec(memory_space=pltpu.SMEM)] + [anywhere] * 5,
        out_specs=(inside, inside, inside),
        scratch_shapes=[
            vm((ROWS, D), BF),
            vm((WCH, D // WCH, KV), BF),
            vm((ROWS, KV), BF),
            vm((NX, ROWS, GW), BF),
            vm((NX, ROWS, GW), BF),
            vm((SEQ, HD), BF),
            vm((SEQ, HD), BF),
            vm((2, NY, NX, ROWS, DH), BF),
            vm((2, NX - 1, NY, ROWS, DH), BF),
            vm((SEQ, HD), F32),
            vm((SEQ, HD), F32),
            vm((GW, HD), BF),
            vm((GW, HD), BF),
            vm((HD, GW), BF),
            vm((HD, GW), BF),
            vm((SEQ, GW), F32),
            vm((SEQ, GW), F32),
            vm((SEQ // KS, 8, GW), F32),
            vm((NY, NX, ROWS, HD), BF),
            vm((NY, NX, ROWS, HD), BF),
            vm((NY - 1, NX, ROWS, HD), BF),
            vm((NY - 1, NX, ROWS, HD), BF),
            vm((NX, ROWS, HD), BF),
            vm((NX, ROWS, HD), BF),
            vm((NY, KV, CK), BF),
            vm((KV, DH), F32),
            vm((2, ND, CB, DH), BF),
            vm((2, ND, CB, DH), BF),
            vm((8, 128), F32),
            vm((NC, 8, 128), F32),
            vm((8, 128), F32),
            vm((ND, 8, 128), F32),
            pltpu.SemaphoreType.DMA((NSEM,)),
            pltpu.SemaphoreType.DMA((NSEM,)),
            pltpu.SemaphoreType.DMA((LW + WCH,)),
        ],
        compiler_params=pltpu.CompilerParams(
            collective_id=0, has_side_effects=True, vmem_limit_bytes=56 * 2**20
        ),
    )(lengths, layer_input[0], value_weight, queries[0], key_states[0], out_grads[0])
    clipped, norm, key_grads = pl.pallas_call(
        finish,
        out_shape=(
            jax.ShapeDtypeStruct((CB, DB), F32),
            jax.ShapeDtypeStruct((1,), F32),
            jax.ShapeDtypeStruct((1, ROWS, KV), BF),
        ),
        in_specs=[inside, pl.BlockSpec(memory_space=pltpu.SMEM), inside],
        out_specs=(inside, pl.BlockSpec(memory_space=pltpu.SMEM), inside),
    )(clipped, norm, key_grads)
    return clipped.T, norm, key_grads

def solution(mesh):
    placed = (
        P("dp", "context", None),
        P(),
        P("dp", "context", None),
        P("dp", "context", None),
        P("dp", "context", None),
        P("dp"),
    )
    return jax.shard_map(
        body,
        mesh=mesh,
        in_specs=placed,
        out_specs=(P("context", "dp"), P("dp"), P("dp", "context", None)),
        check_vma=False,
    )
```

```python
import functools
import math

import jax
import jax.numpy as jnp
from jax import lax
from jax.experimental import pallas as pl
from jax.experimental.pallas import tpu as pltpu
from jax.sharding import PartitionSpec as P

MESH = pl.DeviceIdType.MESH
BF = jnp.bfloat16
F32 = jnp.float32

D = 8192
HD = 128
KV = 512
NX = 4
NY = 4
NC = NX * NY
ND = 16
ROWS = 128
GH = 8
GW = GH * HD
SEQ = NC * ROWS
CK = NY * ROWS
KS = 512
STEPS = CK // KS
DB = D // NC
NH = 1
DH = DB // NH
CB = KV // ND
WCH = 8
SCALE = HD ** (-0.5)
C2 = SCALE * math.log2(math.e)
CLIP = math.sqrt(D * KV)

K1, Q, G, V1, RK, KO, AX, AY = range(0, 32, 4)
K2, V2, XY, XX, AXF, AYF, GR, FC, RV, NM = range(32, 32 + 10 * 32, 32)
NSEM = 352
LX, LQ, LG, LK, LV, LXG, LW = 0, 1, 2, 3, 4, 5, 13


def attend(k, y, length, qb, gb, kf, vf, dk, dv, qs, gs, qt, gt, p_s, d_s, m_s, done):
    q_pos = CK * k + ROWS * y + lax.broadcasted_iota(jnp.int32, (ROWS, HD), 0)
    keep = q_pos < length
    for h in range(GH):
        cols = slice(h * HD, (h + 1) * HD)
        q = qb[k, :, cols]
        g = jnp.where(keep, gb[k, :, cols].astype(F32), 0.0)
        qs[cols, :] = q
        gs[cols, :] = g.astype(BF)
        qt[:, cols] = q.astype(F32).T.astype(BF)
        gt[:, cols] = g.T.astype(BF)

    def sweep_a(j, carry, masked):
        m, l, off = carry
        rows = pl.ds(pl.multiple_of(j * KS, KS), KS)
        s = jnp.dot(kf[rows, :], qt[...], preferred_element_type=F32)
        dp = jnp.dot(vf[rows, :], gt[...], preferred_element_type=F32)
        if masked:
            ki = lax.broadcasted_iota(jnp.int32, (KS, GW), 0)
            qi = lax.broadcasted_iota(jnp.int32, (KS, GW), 1) & (HD - 1)
            s = jnp.where(ki - qi <= CK * k + ROWS * y - KS * j, s, -jnp.inf)
        mn = jnp.maximum(m, jnp.max(s, axis=0, keepdims=True))
        a = jnp.exp2((m - mn) * C2)
        p = jnp.exp2((s - mn) * C2)
        p_s[rows, :] = p
        d_s[rows, :] = dp
        m_s[j] = jnp.broadcast_to(mn, (8, GW))
        l = l * a + jnp.sum(p, axis=0, keepdims=True)
        off = off * a + jnp.sum(p * dp, axis=0, keepdims=True)
        return mn, l, off

    zero = jnp.zeros((1, GW), F32)
    carry = (jnp.full((1, GW), -jnp.inf, F32), zero, zero)
    carry = lax.fori_loop(0, k * STEPS, lambda j, c: sweep_a(j, c, False), carry)
    for t in range(STEPS):
        carry = sweep_a(k * STEPS + t, carry, True)
    m, l, off = carry
    inv = 1.0 / l
    off = off * inv

    def sweep_b(j, _):
        rows = pl.ds(pl.multiple_of(j * KS, KS), KS)
        p = p_s[rows, :] * (jnp.exp2((m_s[j][0:1] - m) * C2) * inv)
        ds = p * (d_s[rows, :] - off)
        dv[rows, :] += jnp.dot(p.astype(BF), gs[...], preferred_element_type=F32)
        dk[rows, :] += jnp.dot(ds.astype(BF), qs[...], preferred_element_type=F32)
        if done:
            done(j)
        return 0

    lax.fori_loop(0, (k + 1) * STEPS, sweep_b, 0)


def kernel(
    len_ref, x_ref, w_ref, q_ref, k_ref, g_ref,
    cs_ref, nm_ref, kg_ref,
    xv, wv, vown, qb, gb, kf, vf, xg, xs, dk, dv, qs, gs, qt, gt, p_s, d_s, m_s,
    dvs, dks, dvr, dkr, kout, kin, dvt, acc, gsend, gr, nsend, nr, fsend, fr,
    send, recv, local,
):
    c = lax.axis_index("context")
    d = lax.axis_index("dp")
    x, y = c // NY, lax.rem(c, NY)
    length = len_ref[0]
    sent = []

    def at_x(o):
        return lax.rem(x + o, NX)

    def at_y(o):
        return lax.rem(y + o, NY)

    def remote(src, dst, sem, **peer):
        copy = pltpu.make_async_remote_copy(
            src_ref=src, dst_ref=dst, send_sem=send.at[sem], recv_sem=recv.at[sem],
            device_id=peer, device_id_type=MESH,
        )
        copy.start()
        sent.append(copy)
        return copy

    def near(src, dst, sem):
        copy = pltpu.make_async_copy(src, dst, local.at[sem])
        copy.start()
        return copy

    def cols(index, width):
        return pl.ds(pl.multiple_of(index * width, width), width)

    def place(ref, xi, yi):
        return ref.at[cols(xi * NY + yi, ROWS), :]

    load_x = near(x_ref, xv, LX)
    load_w = [near(w_ref.at[pl.ds(i * (D // WCH), D // WCH), :], wv.at[i], LW + i) for i in range(WCH)]
    own = [
        near(k_ref.at[:, cols(x, HD)], place(kf, x, y), LK),
        near(q_ref.at[:, cols(x, GW)], qb.at[x], LQ),
        near(g_ref.at[:, cols(x, GW)], gb.at[x], LG),
    ]

    def staged(h, i, yi):
        return xs.at[h, i - 1, yi] if i else xg.at[h, yi, x]

    def input_cols(h, there):
        return x_ref.at[:, pl.ds(pl.multiple_of(there * DB + h * DH, DH), DH)]

    for h in range(NH):
        for i in range(NX):
            src = input_cols(h, at_x(i) * NY + y)
            own.append(near(src, staged(h, i, y), LXG + NX * h + i))

    def on_x(o):
        return {"context": at_x(o) * NY + y}

    def on_y(o):
        return {"context": x * NY + at_y(o)}

    def on_dp(o):
        return {"dp": lax.rem(d + o, ND)}

    def on_xy(i, j):
        return {"context": at_x(i) * NY + at_y(j)}

    barrier = pltpu.get_barrier_semaphore()
    others = [(i, j) for i in range(NX) for j in range(NY) if i or j]
    peers = [on_xy(i, j) for i, j in others] + [on_dp(o) for o in range(1, ND)]
    for peer in peers:
        pl.semaphore_signal(barrier, inc=1, device_id=peer, device_id_type=MESH)

    dk[...] = jnp.zeros_like(dk)
    dv[...] = jnp.zeros_like(dv)
    load_x.wait()
    total = jnp.zeros((ROWS, KV), F32)
    for i in range(WCH):
        load_w[i].wait()
        part = xv[:, i * (D // WCH) : (i + 1) * (D // WCH)]
        total += jnp.dot(part, wv[i], preferred_element_type=F32)
    vown[...] = total.astype(BF)
    v_own = near(vown.at[:, cols(x, HD)], place(vf, x, y), LV)

    pl.semaphore_wait(barrier, len(peers))

    v1 = [
        remote(vown.at[:, cols(at_x(o), HD)], place(vf, x, y), V1 + o, **on_x(o))
        for o in range(1, NX)
    ]
    k1 = [
        remote(k_ref.at[:, cols(at_x(o), HD)], place(kf, x, y), K1 + o, **on_x(o))
        for o in range(1, NX)
    ]
    qc, gc = {}, {}

    def queries_x(o):
        qc[o] = remote(q_ref.at[:, cols(at_x(o), GW)], qb.at[x], Q + o, **on_x(o))

    def grads_x(o):
        gc[o] = remote(g_ref.at[:, cols(at_x(o), GW)], gb.at[x], G + o, **on_x(o))

    queries_x(1)
    queries_x(3)

    def gather_y(ref, sem):
        copies = []
        for o in range(1, NY):
            for i in range(NX):
                copies.append(
                    remote(place(ref, i, y), place(ref, i, y), sem + NX * o + i, **on_y(o))
                )
        return copies

    own[0].wait()
    for copy in k1:
        copy.wait_recv()
    k2 = gather_y(kf, K2)

    v_own.wait()
    for copy in v1:
        copy.wait_recv()
    v2 = gather_y(vf, V2)
    grads_x(1)
    grads_x(3)
    queries_x(2)
    grads_x(2)

    xy, xx = {}, {}

    def input_y(h, i):
        for o in range(1, NY):
            src = input_cols(h, at_x(i) * NY + at_y(o))
            sem = XY + NC * h + NX * o + i
            xy[h, i, o] = remote(src, staged(h, i, y), sem, **on_y(o))

    def input_x(h, i):
        own[3 + NX * h + i].wait()
        for o in range(1, NY):
            xy[h, i, o].wait_recv()
        if i:
            xx[h, i] = remote(xs.at[h, i - 1], xg.at[h, :, x], XX + NX * h + i, **on_x(i))

    for i in (1, 3, 2, 0):
        input_y(0, i)
    for copy in k2 + v2:
        copy.wait_recv()
    def sum_copy(o, j):
        sem = RV + NX * o + j
        return pltpu.make_async_remote_copy(
            src_ref=dvs.at[at_y(o), j], dst_ref=dvr.at[o - 1, j], send_sem=send.at[sem],
            recv_sem=recv.at[sem], device_id=on_y(o), device_id_type=MESH,
        )

    def sum_start(j):
        for yy in range(NY):
            dvs[yy, j] = dv[cols(j * NY + yy, ROWS), :].astype(BF)
        for o in range(1, NY):
            sum_copy(o, j).start()
        return 0

    for o in (0, 1, 3, 2):
        if o:
            qc[o].wait_recv()
            gc[o].wait_recv()
        else:
            own[1].wait()
            own[2].wait()
        k = lax.rem(x + NX - o, NX)
        done = None
        if o == 2:
            done = sum_start
            lax.fori_loop(k + 1, NX, lambda j, _: sum_start(j), 0)
        attend(k, y, length, qb, gb, kf, vf, dk, dv, qs, gs, qt, gt, p_s, d_s, m_s, done)
        if o == 1:
            input_x(0, 1)
            input_x(0, 3)
        elif o == 3:
            input_x(0, 2)

    def split_y(ref, out, got, sem, scale):
        for yy in range(NY):
            for j in range(NX):
                block = ref[(j * NY + yy) * ROWS : (j * NY + yy + 1) * ROWS, :]
                out[yy, j] = (block * scale).astype(BF) if scale else block.astype(BF)
        return [
            remote(out.at[at_y(o)], got.at[o - 1], sem + o, **on_y(o))
            for o in range(1, NY)
        ]

    def summed(ref, got, j, scale):
        block = ref[cols(j * NY + y, ROWS), :]
        if scale:
            block = block * scale
        for o in range(1, NY):
            block = block + got[o - 1, j].astype(F32)
        return block

    rv = [sum_copy(o, j) for j in range(NX) for o in range(1, NY)]
    sent.extend(rv)
    for copy in rv:
        copy.wait_recv()
    for j in range(NX):
        dvt[y, cols(x, HD), j * ROWS : (j + 1) * ROWS] = summed(dv, dvr, j, None).T.astype(BF)
    half = CK // 2
    part = dvt.at[y, cols(x, HD), :]
    ax, ay, axf, ayf = {}, {}, {}, {}
    for o in (1, 3, 2):
        ax[o] = remote(part, part, AX + o, **on_x(o))
        ay[o] = remote(part, part, AY + o, **on_y(o))
    for o in (1, 3, 2):
        ax[o].wait_recv()
        part = dvt.at[y, cols(lax.rem(x + NX - o, NX), HD), half:]
        for j in (1, 3, 2):
            ayf[o, j] = remote(part, part, AYF + NY * o + j, **on_y(j))
        ay[o].wait_recv()
        part = dvt.at[lax.rem(y + NY - o, NY), cols(x, HD), :half]
        for i in (1, 3, 2):
            axf[i, o] = remote(part, part, AXF + NY * i + o, **on_x(i))
    rk = split_y(dk, dks, dkr, RK, SCALE)

    squares = jnp.zeros((1, 1), F32)
    gx = []
    for h in range(NH):
        input_x(h, 0)
        for i in range(1, NX):
            xx[h, i].wait_recv()
        for j in (0, 1, 3, 2):
            if h == 0:
                for i in range(1, NX):
                    if j:
                        axf[i, j].wait_recv()
                        ayf[i, j].wait_recv()
            yy = lax.rem(y + NY - j, NY)
            part = jnp.dot(dvt[yy], xg[h, yy].reshape(CK, DH), preferred_element_type=F32)
            acc[...] = acc[...] + part if j else part
        total = acc[...]
        for i in range(ND):
            gsend[h, i] = total[i * CB : (i + 1) * CB, :].astype(BF)
        gr[h, d] = gsend[h, d]
        for o in range(1, ND):
            there = lax.rem(d + o, ND)
            gx.append(remote(gsend.at[h, there], gr.at[h, d], GR + ND * h + o, **on_dp(o)))
        columns = jnp.sum(total * total, axis=0, keepdims=True)
        squares = squares + jnp.sum(columns, axis=1, keepdims=True)
    nsend[...] = jnp.broadcast_to(squares, (8, 128))
    nx = [remote(nsend, nr.at[c], NM + NY * i + j, **on_xy(i, j)) for i, j in others]
    nr[c] = nsend[...]
    for copy in nx:
        copy.wait_recv()
    squares = nr[0]
    for i in range(1, NC):
        squares = squares + nr[i]
    norm = jnp.sqrt(squares)
    nm_ref[...] = norm
    fsend[...] = CLIP / (norm + 0.01)
    fx = [
        remote(fsend, fr.at[d], FC + o, **on_dp(o)) for o in range(1, ND)
    ]
    fr[d] = fsend[...]

    for copy in rk:
        copy.wait_recv()
    for j in range(NX):
        kout[j] = summed(dk, dkr, j, SCALE).astype(BF)
    kin[x] = kout[x]
    ko = [
        remote(kout.at[at_x(o)], kin.at[x], KO + o, **on_x(o)) for o in range(1, NX)
    ]
    for copy in ko:
        copy.wait_recv()
    for i in range(NX):
        kg_ref[:, i * HD : (i + 1) * HD] = kin[i]

    for copy in fx + gx:
        copy.wait_recv()
    for h in range(NH):
        clipped = fr[0][0:1, 0:1] * gr[h, 0].astype(F32)
        for i in range(1, ND):
            clipped = clipped + fr[i][0:1, 0:1] * gr[h, i].astype(F32)
        cs_ref[:, h * DH : (h + 1) * DH] = clipped

    for copy in sent:
        copy.wait_send()


def finish(clipped_ref, norm_ref, key_ref, cs_ref, nm_ref, kg_ref):
    cs_ref[...] = clipped_ref[...]
    nm_ref[0] = norm_ref[0, 0]
    kg_ref[0] = key_ref[...]


def body(layer_input, value_weight, queries, key_states, out_grads, lengths):
    vm = pltpu.VMEM
    anywhere = pl.BlockSpec(memory_space=pl.ANY)
    inside = pl.BlockSpec(memory_space=pltpu.VMEM)
    clipped, norm, key_grads = pl.pallas_call(
        kernel,
        out_shape=(
            jax.ShapeDtypeStruct((CB, DB), F32),
            jax.ShapeDtypeStruct((8, 128), F32),
            jax.ShapeDtypeStruct((ROWS, KV), BF),
        ),
        in_specs=[pl.BlockSpec(memory_space=pltpu.SMEM)] + [anywhere] * 5,
        out_specs=(inside, inside, inside),
        scratch_shapes=[
            vm((ROWS, D), BF),
            vm((WCH, D // WCH, KV), BF),
            vm((ROWS, KV), BF),
            vm((NX, ROWS, GW), BF),
            vm((NX, ROWS, GW), BF),
            vm((SEQ, HD), BF),
            vm((SEQ, HD), BF),
            vm((NH, NY, NX, ROWS, DH), BF),
            vm((NH, NX - 1, NY, ROWS, DH), BF),
            vm((SEQ, HD), F32),
            vm((SEQ, HD), F32),
            vm((GW, HD), BF),
            vm((GW, HD), BF),
            vm((HD, GW), BF),
            vm((HD, GW), BF),
            vm((SEQ, GW), F32),
            vm((SEQ, GW), F32),
            vm((SEQ // KS, 8, GW), F32),
            vm((NY, NX, ROWS, HD), BF),
            vm((NY, NX, ROWS, HD), BF),
            vm((NY - 1, NX, ROWS, HD), BF),
            vm((NY - 1, NX, ROWS, HD), BF),
            vm((NX, ROWS, HD), BF),
            vm((NX, ROWS, HD), BF),
            vm((NY, KV, CK), BF),
            vm((KV, DH), F32),
            vm((NH, ND, CB, DH), BF),
            vm((NH, ND, CB, DH), BF),
            vm((8, 128), F32),
            vm((NC, 8, 128), F32),
            vm((8, 128), F32),
            vm((ND, 8, 128), F32),
            pltpu.SemaphoreType.DMA((NSEM,)),
            pltpu.SemaphoreType.DMA((NSEM,)),
            pltpu.SemaphoreType.DMA((LW + WCH,)),
        ],
        compiler_params=pltpu.CompilerParams(
            collective_id=0, has_side_effects=True, vmem_limit_bytes=56 * 2**20
        ),
    )(lengths, layer_input[0], value_weight, queries[0], key_states[0], out_grads[0])
    clipped, norm, key_grads = pl.pallas_call(
        finish,
        out_shape=(
            jax.ShapeDtypeStruct((CB, DB), F32),
            jax.ShapeDtypeStruct((1,), F32),
            jax.ShapeDtypeStruct((1, ROWS, KV), BF),
        ),
        in_specs=[inside, pl.BlockSpec(memory_space=pltpu.SMEM), inside],
        out_specs=(inside, pl.BlockSpec(memory_space=pltpu.SMEM), inside),
    )(clipped, norm, key_grads)
    return clipped.T, norm, key_grads


def solution(mesh):
    placed = (
        P("dp", "context", None),
        P(),
        P("dp", "context", None),
        P("dp", "context", None),
        P("dp", "context", None),
        P("dp"),
    )
    return jax.shard_map(
        body,
        mesh=mesh,
        in_specs=placed,
        out_specs=(P("context", "dp"), P("dp"), P("dp", "context", None)),
        check_vma=False,
    )
```
